1024 devices in a mesh: blk: 32 (over y, z_hi, core), narrow: 32 (over x, z_lo).
Axes of the slice: x: 4, y: 8, z: 16 (z_hi: 2, z_lo: 8; z = z_hi * 8 + z_lo), core: 2. Of those that a mesh axis runs over, the one named last changes fastest.
Arguments:
- image_emb: bfloat16 [262144, 1152], P(('blk', 'narrow')), as said below
- text_emb: bfloat16 [262144, 1152], P(('blk', 'narrow')), as said below
- partner: int32 [1024, 256], P(('blk', 'narrow')), may hold values from 0 to 255, each once within a row
- scale: float32 [1], replicated, may hold values from 60 to 120
- bias: float32 [1], replicated, may hold values from -4 to 0
Outputs:
- row_loss: float32 [262144], P(('blk', 'narrow'))
- grad_image: bfloat16 [262144, 1152], P(('blk', 'narrow'))
- grad_text: bfloat16 [262144, 1152], P(('blk', 'narrow'))
The draws below stay inside these ranges and needn't reach their ends.
Inputs may be any that keep to these rules, and one draw needn't show every extreme that they name: Each row of partner is an ordering of 0 to 255. `image_emb`: embeddings as the towers emit them, before normalization. `text_emb`: embeddings as the towers emit them, before normalization.
All inputs are finite; a program needn't handle non-finite values.
Results may differ from the reference program's by a relative error of at most 0.01.
Values may be sent and summed in bfloat16 or wider, within the bound.
No kernel may reach another device: no remote copies, remote signals or barrier semaphores. Data moves between devices by JAX's collectives and lax.ppermute only.
A program may use at most 32 MiB of HBM per device.

```python
import math
import jax
import jax.numpy as jnp
from jax import lax

D = 1152
ROWS = 256
SPANS = 4
BLOCKS = 1024
ROWS_ALL = 262144
N_BLK = 32
N_NARROW = 32


def tower_rows(key, low, high):
    first, second = jax.random.split(key, 2)
    count = ROWS_ALL
    spread = jnp.exp(jax.random.uniform(second, (count, 1), jnp.float32, math.log(low), math.log(high)))
    base = jax.random.normal(first, (count, D), jnp.float32)
    return (base * spread).astype(jnp.bfloat16)


def draw_image_emb(key, part):
    key = jax.random.fold_in(key, 11)
    return tower_rows(key, 0.3, 3.0)


def draw_text_emb(key, part):
    key = jax.random.fold_in(key, 23)
    return tower_rows(key, 0.3, 3.0)


def setup_inputs(seed: int = 0) -> dict:
    seeds = jax.random.split(jax.random.key(seed), 6)
    image_emb = draw_image_emb(jax.random.fold_in(seeds[5], 71), 0)
    text_emb = draw_text_emb(jax.random.fold_in(seeds[5], 71), 0)
    partner = jax.vmap(lambda own: jax.random.permutation(own, ROWS))(jax.random.split(seeds[2], BLOCKS)).reshape((BLOCKS, ROWS)).astype(jnp.int32)
    scale = jnp.clip(jax.random.uniform(seeds[3], (1,), jnp.float32, 60.0, 120.0), 60.0, 120.0)
    bias = jnp.clip(jax.random.uniform(seeds[4], (1,), jnp.float32, -4.0, 0.0), -4.0, 0.0)
    return {"image_emb": image_emb, "text_emb": text_emb, "partner": partner, "scale": scale, "bias": bias}


EPS = 1e-06

def unit_rows(raw):
    values = raw.astype(jnp.float32)
    norm = jnp.sqrt(lax.optimization_barrier(jnp.sum(values * values, axis=-1, keepdims=True)) + EPS)
    return (values / norm, norm)

def project_back(direction, grad_unit, norm):
    along = lax.optimization_barrier(jnp.sum(direction * grad_unit, axis=-1, keepdims=True))
    return ((grad_unit - direction * along) / norm).astype(jnp.bfloat16)

def reference(image_emb, text_emb, partner, scale, bias):
    image_dir, image_norm = unit_rows(image_emb)
    text_dir, text_norm = unit_rows(text_emb)
    shape4 = (N_BLK, N_NARROW, ROWS, D)
    image_unit = image_dir.astype(jnp.bfloat16).reshape(shape4)
    text_unit = text_dir.astype(jnp.bfloat16).reshape(shape4)
    pairing = partner.reshape(N_BLK, N_NARROW, ROWS)
    factor = scale[0]
    offset = bias[0]
    columns = jnp.arange(ROWS, dtype=jnp.int32)
    texts = [text_unit, jnp.roll(text_unit, 1, axis=0), jnp.roll(text_unit, 2, axis=0), jnp.roll(jnp.roll(text_unit, 2, axis=0), 1, axis=1)]
    loss_total = jnp.zeros((N_BLK, N_NARROW, ROWS), jnp.float32)
    grad_img = jnp.zeros(shape4, jnp.float32)
    grad_txt = jnp.zeros(shape4, jnp.float32)
    for which in range(4):

        def per_block(items, which=which):
            left, right, pairs = items
            left32 = left.astype(jnp.float32)
            right32 = right.astype(jnp.float32)
            logit = factor * jnp.einsum('nid,njd->nij', left32, right32) + offset
            if which == 0:
                sign = jnp.where(pairs[:, :, None] == columns[None, None, :], 1.0, -1.0).astype(jnp.float32)
            else:
                sign = -jnp.ones(logit.shape, jnp.float32)
            pair_loss = jax.nn.softplus(-sign * logit)
            weight = (-sign * jax.nn.sigmoid(-sign * logit) / SPANS).astype(jnp.bfloat16).astype(jnp.float32)
            d_left = factor * jnp.einsum('nij,njd->nid', weight, right32)
            d_right = factor * jnp.einsum('nij,nid->njd', weight, left32)
            return (lax.optimization_barrier(jnp.sum(pair_loss, axis=-1)), d_left, d_right)
        part_loss, d_left, d_right = lax.map(per_block, (image_unit, texts[which], pairing))
        loss_total = loss_total + part_loss
        grad_img = grad_img + d_left
        if which == 0:
            grad_txt = grad_txt + d_right
        elif which == 1:
            grad_txt = grad_txt + jnp.roll(d_right, -1, axis=0)
        elif which == 2:
            grad_txt = grad_txt + jnp.roll(d_right, -2, axis=0)
        else:
            grad_txt = grad_txt + jnp.roll(jnp.roll(d_right, -2, axis=0), -1, axis=1)
    row_loss = (loss_total / (SPANS * ROWS)).reshape(ROWS_ALL)
    grad_image = project_back(image_dir, grad_img.reshape(ROWS_ALL, D), image_norm)
    grad_text = project_back(text_dir, grad_txt.reshape(ROWS_ALL, D), text_norm)
    return (row_loss, grad_image, grad_text)
```

```python
import jax
import jax.numpy as jnp
from jax import lax
from jax.sharding import PartitionSpec as P

SPANS = 4
EPS = 1e-06
AXES = ("blk", "narrow")


def moved(block, target):
    rows, cols = lax.axis_size("blk"), lax.axis_size("narrow")
    route = []
    for b in range(rows):
        for n in range(cols):
            to_b, to_n = target(b, n)
            route.append((b * cols + n, (to_b % rows) * cols + to_n % cols))
    return lax.ppermute(block, AXES, route)


def unit_rows(raw):
    values = raw.astype(jnp.float32)
    norm = jnp.sqrt(jnp.sum(values * values, axis=-1, keepdims=True) + EPS)
    return (values / norm, norm)


def unit16(raw):
    return unit_rows(raw)[0].astype(jnp.bfloat16)


def project_back(direction, grad_unit, norm):
    along = jnp.sum(direction * grad_unit, axis=-1, keepdims=True)
    return ((grad_unit - direction * along) / norm).astype(jnp.bfloat16)


def gram(a, b):
    return lax.dot_general(a, b, (((1,), (1,)), ((), ())), preferred_element_type=jnp.float32)


def weights(logit, positive):
    if positive is None:
        signed = logit
        weight = jax.nn.sigmoid(logit) / SPANS
    else:
        sign = jnp.where(positive, 1.0, -1.0).astype(jnp.float32)
        signed = -sign * logit
        weight = -sign * jax.nn.sigmoid(signed) / SPANS
    return weight.astype(jnp.bfloat16), signed


def local(image_emb, text_emb, partner, scale, bias):
    factor, offset = scale[0], bias[0]
    even = lax.axis_index("blk") % 2 == 0
    text_1 = moved(text_emb, lambda b, n: (b + 2, n + 1))
    image_1 = moved(image_emb, lambda b, n: (b - 2, n - 1))
    text_2 = moved(text_1, lambda b, n: (b, n - 1))
    image_2 = moved(image_1, lambda b, n: (b, n + 1))
    text_3 = moved(jnp.where(even, text_emb, text_2), lambda b, n: (b ^ 1, n))
    image_3 = moved(jnp.where(even, image_2, image_emb), lambda b, n: (b ^ 1, n))

    image_dir, image_norm = unit_rows(image_emb)
    text_dir, text_norm = unit_rows(text_emb)
    image_unit = image_dir.astype(jnp.bfloat16)
    text_unit = text_dir.astype(jnp.bfloat16)
    count = image_unit.shape[0]
    positive = partner[0][:, None] == lax.broadcasted_iota(jnp.int32, (count, count), 1)

    own, signed = weights(factor * gram(image_unit, text_unit) + offset, positive)
    loss = jnp.sum(jax.nn.softplus(signed), axis=-1)
    grad_img = jnp.dot(own, text_unit, preferred_element_type=jnp.float32)
    grad_txt = lax.dot_general(
        own, image_unit, (((0,), (0,)), ((), ())), preferred_element_type=jnp.float32
    )
    for raw in (text_1, text_2, text_3):
        other = unit16(raw)
        weight, signed = weights(factor * gram(image_unit, other) + offset, None)
        loss = loss + jnp.sum(jax.nn.softplus(signed), axis=-1)
        grad_img = grad_img + jnp.dot(weight, other, preferred_element_type=jnp.float32)
    for raw in (image_1, image_2, image_3):
        other = unit16(raw)
        weight, _ = weights(factor * gram(text_unit, other) + offset, None)
        grad_txt = grad_txt + jnp.dot(weight, other, preferred_element_type=jnp.float32)

    row_loss = loss / (SPANS * count)
    grad_image = project_back(image_dir, factor * grad_img, image_norm)
    grad_text = project_back(text_dir, factor * grad_txt, text_norm)
    return (row_loss, grad_image, grad_text)


def solution(mesh):
    rows = P(AXES, None)
    return jax.shard_map(
        local,
        mesh=mesh,
        in_specs=(rows, rows, rows, P(), P()),
        out_specs=(P(AXES), rows, rows),
        check_vma=False,
    )
```

```python
import jax
import jax.numpy as jnp
from jax import lax
from jax.experimental import pallas as pl
from jax.experimental.pallas import tpu as pltpu
from jax.sharding import PartitionSpec as P

SPANS = 4
EPS = 1e-06
AXES = ("blk", "narrow")
F32 = jnp.float32
BF16 = jnp.bfloat16


def moved(block, target):
    rows, cols = lax.axis_size("blk"), lax.axis_size("narrow")
    route = []
    for b in range(rows):
        for n in range(cols):
            to_b, to_n = target(b, n)
            route.append((b * cols + n, (to_b % rows) * cols + to_n % cols))
    return lax.ppermute(block, AXES, route)


def x_far(b, n):
    return (b + 2, n + 1) if b % 2 else (b - 2, n - 1)


def x_near(b, n):
    return (b, n - 1) if b % 2 else (b, n + 1)


def y_far(b, n):
    return (b - 2, n - 1) if b % 2 else (b + 2, n + 1)


def y_near(b, n):
    return (b, n + 1) if b % 2 else (b, n - 1)


def sibling(b, n):
    return (b ^ 1, n)


def to_unit(values):
    norm = jnp.sqrt(jnp.sum(values * values, axis=-1, keepdims=True) + EPS)
    return (values * (1.0 / norm)).astype(BF16), norm


def terms(fixed, other, factor, offset, positive=None):
    logit = factor * lax.dot_general(
        fixed, other, (((1,), (1,)), ((), ())), preferred_element_type=F32
    ) + offset
    signed = logit if positive is None else jnp.where(positive, -logit, logit)
    small = jnp.exp(-jnp.abs(signed))
    loss = jnp.maximum(signed, 0.0) + jnp.log1p(small)
    share = 1.0 / (1.0 + small)
    weight = jnp.where(signed >= 0.0, share, small * share) * (1.0 / SPANS)
    if positive is not None:
        weight = jnp.where(positive, -weight, weight)
    grad = jnp.dot(weight.astype(BF16), other, preferred_element_type=F32)
    return jnp.sum(loss, axis=-1, keepdims=True), grad


def project(unit_source, norm, grad_unit):
    direction = unit_source * (1.0 / norm)
    along = jnp.sum(direction * grad_unit, axis=-1, keepdims=True)
    return ((grad_unit - direction * along) * (1.0 / norm)).astype(BF16)


def own_kernel(flags, scalars, u, v, e, pcol, prow, uu, vu, un, vn, gu, gv, lu, lv):
    factor, offset = scalars[0], scalars[1]
    even = flags[0] == 1
    u_unit, u_norm = to_unit(u[...].astype(F32))
    v_unit, v_norm = to_unit(v[...].astype(F32))
    shape = (u.shape[0], v.shape[0])
    by_col = pcol[...] - lax.broadcasted_iota(jnp.int32, shape, 1)
    by_row = prow[...] - lax.broadcasted_iota(jnp.int32, shape, 0)
    loss_u, grad_u = terms(u_unit, v_unit, factor, offset, jnp.where(even, by_col, by_row) == 0)
    loss_v, grad_v = terms(v_unit, u_unit, factor, offset, jnp.where(even, by_row, by_col) == 0)
    e_unit, _ = to_unit(e[...].astype(F32))
    loss_e, grad_e = terms(v_unit, e_unit, factor, offset)
    uu[...] = u_unit
    vu[...] = v_unit
    un[...] = u_norm
    vn[...] = v_norm
    gu[...] = grad_u
    gv[...] = grad_v + grad_e
    lu[...] = loss_u
    lv[...] = loss_v + loss_e


def far_kernel(flags, scalars, xc, yc, uu, vu, gu, gv, lu, lv, gu2, gv2, lu2, lv2):
    factor, offset = scalars[0], scalars[1]
    x_unit, _ = to_unit(xc[...].astype(F32))
    loss, grad = terms(vu[...], x_unit, factor, offset)
    gv2[...] = gv[...] + grad
    lv2[...] = lv[...] + loss
    y_unit, _ = to_unit(yc[...].astype(F32))
    loss, grad = terms(uu[...], y_unit, factor, offset)
    gu2[...] = gu[...] + grad
    lu2[...] = lu[...] + loss


def near_kernel(flags, scalars, xd, v, vn, vu, gv, lv, out_v, lv2):
    factor, offset = scalars[0], scalars[1]
    x_unit, _ = to_unit(xd[...].astype(F32))
    loss, grad = terms(vu[...], x_unit, factor, offset)
    lv2[...] = lv[...] + loss
    out_v[...] = project(v[...].astype(F32), vn[...], factor * (gv[...] + grad))


def last_kernel(flags, scalars, yd, sib, u, un, uu, gu, lu, lv, out_v, loss_out, image_out, text_out):
    factor, offset = scalars[0], scalars[1]
    even = flags[0] == 1
    y_unit, _ = to_unit(yd[...].astype(F32))
    loss_y, grad_y = terms(uu[...], y_unit, factor, offset)
    s_unit, _ = to_unit(sib[...].astype(F32))
    loss_s, grad_s = terms(uu[...], s_unit, factor, offset)
    out_u = project(u[...].astype(F32), un[...], factor * (gu[...] + grad_y + grad_s))
    row_loss = jnp.where(even, lu[...] + loss_y + loss_s, lv[...])
    row_loss = row_loss * (1.0 / (SPANS * u.shape[0]))
    loss_out[...] = jnp.broadcast_to(row_loss, (row_loss.shape[0], 128)).T[0:1, :]

    @pl.when(even)
    def _():
        image_out[...] = out_u
        text_out[...] = out_v[...]

    @pl.when(jnp.logical_not(even))
    def _():
        image_out[...] = out_v[...]
        text_out[...] = out_u


def call(kernel, outs, pairs, *args, weight=1):
    smem = pl.BlockSpec(memory_space=pltpu.SMEM)
    vmem = pl.BlockSpec(memory_space=pltpu.VMEM)
    rows, depth = 256, 1152
    return pl.pallas_call(
        kernel,
        out_shape=outs,
        in_specs=[smem, smem] + [vmem] * (len(args) - 2),
        out_specs=[vmem] * len(outs),
        compiler_params=pltpu.CompilerParams(vmem_limit_bytes=32 * 2**20),
        cost_estimate=pl.CostEstimate(
            flops=4 * weight * pairs * rows * rows * depth,
            bytes_accessed=8 * rows * depth * 2,
            transcendentals=2 * pairs * rows * rows,
        ),
    )(*args)


def local(image_emb, text_emb, partner, scale, bias):
    rows, depth = image_emb.shape
    even = lax.axis_index("blk") % 2 == 0
    flags = even.astype(jnp.int32).reshape(1)
    scalars = jnp.concatenate([scale, bias])
    u = jnp.where(even, image_emb, text_emb)
    v = jnp.where(even, text_emb, image_emb)
    half = jax.ShapeDtypeStruct((rows, depth), BF16)
    full = jax.ShapeDtypeStruct((rows, depth), F32)
    col = jax.ShapeDtypeStruct((rows, 1), F32)

    xc = moved(u, x_far)
    yc = moved(v, y_far)
    e = moved(v, sibling)
    uu, vu, un, vn, gu, gv, lu, lv = call(
        own_kernel, (half, half, col, col, full, full, col, col), 3,
        flags, scalars, u, v, e, partner.reshape(rows, 1), partner, weight=10,
    )
    xc, gv = lax.optimization_barrier((xc, gv))
    xd = moved(xc, x_near)
    yd = moved(yc, y_near)
    gu, gv, lu, lv = call(
        far_kernel, (full, full, col, col), 2,
        flags, scalars, xc, yc, uu, vu, gu, gv, lu, lv, weight=10,
    )
    xd, gu = lax.optimization_barrier((xd, gu))
    s = moved(xd, sibling)
    out_v, lv = call(
        near_kernel, (half, col), 1, flags, scalars, xd, v, vn, vu, gv, lv, weight=1
    )
    row_loss, grad_image, grad_text = call(
        last_kernel, (jax.ShapeDtypeStruct((1, rows), F32), half, half), 2,
        flags, scalars, yd, s, u, un, uu, gu, lu, lv, out_v,
    )
    return row_loss.reshape(rows), grad_image, grad_text


def solution(mesh):
    rows = P(AXES, None)
    return jax.shard_map(
        local,
        mesh=mesh,
        in_specs=(rows, rows, rows, P(), P()),
        out_specs=(P(AXES), rows, rows),
        check_vma=False,
    )
```

```python
import jax
import jax.numpy as jnp
from jax import lax
from jax.experimental import pallas as pl
from jax.experimental.pallas import tpu as pltpu
from jax.sharding import PartitionSpec as P

SPANS = 4
EPS = 1e-06
AXES = ("blk", "narrow")
F32 = jnp.float32
BF16 = jnp.bfloat16


def moved(block, target):
    rows, cols = lax.axis_size("blk"), lax.axis_size("narrow")
    route = []
    for b in range(rows):
        for n in range(cols):
            to = target(b, n)
            if to is not None:
                route.append((b * cols + n, (to[0] % rows) * cols + to[1] % cols))
    return lax.ppermute(block, AXES, route)


def text_far(b, n):
    return (b + 2, n + 1)


def text_near(b, n):
    return (b, n - 1)


def image_far(b, n):
    return (b - 2, n - 1)


def image_near(b, n):
    return (b, n + 1)


def sibling(b, n):
    return (b ^ 1, n)


def text_pass(b, n):
    return (b - 1, n) if b % 2 else None


def image_pass(b, n):
    return None if b % 2 else (b + 1, n)


def to_unit(values):
    norm = jnp.sqrt(jnp.sum(values * values, axis=-1, keepdims=True) + EPS)
    return (values * (1.0 / norm)).astype(BF16), norm


def terms(fixed, other, factor, offset, positive=None):
    logit = factor * lax.dot_general(
        fixed, other, (((1,), (1,)), ((), ())), preferred_element_type=F32
    ) + offset
    signed = logit if positive is None else jnp.where(positive, -logit, logit)
    small = jnp.exp(-jnp.abs(signed))
    loss = jnp.maximum(signed, 0.0) + jnp.log1p(small)
    share = 1.0 / (1.0 + small)
    weight = jnp.where(signed >= 0.0, share, small * share) * (1.0 / SPANS)
    if positive is not None:
        weight = jnp.where(positive, -weight, weight)
    grad = jnp.dot(weight.astype(BF16), other, preferred_element_type=F32)
    return jnp.sum(loss, axis=-1, keepdims=True), grad


def project(unit_source, norm, grad_unit):
    direction = unit_source * (1.0 / norm)
    along = jnp.sum(direction * grad_unit, axis=-1, keepdims=True)
    return ((grad_unit - direction * along) * (1.0 / norm)).astype(BF16)


def own_kernel(
    flags, scalars, image, text, pcol, prow, iu, tu, eu, inorm, tnorm, gi, gt, loss_out
):
    factor, offset = scalars[0], scalars[1]
    even = flags[0] == 1
    i_unit, i_norm = to_unit(image[...].astype(F32))
    t_unit, t_norm = to_unit(text[...].astype(F32))
    shape = (image.shape[0], text.shape[0])
    own = pcol[...] == lax.broadcasted_iota(jnp.int32, shape, 1)
    loss, grad = terms(i_unit, t_unit, factor, offset, own)
    loss_out[...] = loss
    gi[...] = grad
    own = prow[...] == lax.broadcasted_iota(jnp.int32, shape, 0)
    gt[...] = terms(t_unit, i_unit, factor, offset, own)[1]
    iu[...] = i_unit
    tu[...] = t_unit
    inorm[...] = i_norm
    tnorm[...] = t_norm

    @pl.when(even)
    def _():
        eu[...] = t_unit

    @pl.when(jnp.logical_not(even))
    def _():
        eu[...] = i_unit


def far_kernel(flags, scalars, t1, i1, iu, tu, gi, gt, loss_in, gi2, gt2, loss_out):
    factor, offset = scalars[0], scalars[1]
    loss, grad = terms(iu[...], to_unit(t1[...].astype(F32))[0], factor, offset)
    gi2[...] = gi[...] + grad
    loss_out[...] = loss_in[...] + loss
    gt2[...] = gt[...] + terms(tu[...], to_unit(i1[...].astype(F32))[0], factor, offset)[1]


def image_kernel(flags, scalars, i2, tu, gt, gt2):
    factor, offset = scalars[0], scalars[1]
    gt2[...] = gt[...] + terms(tu[...], to_unit(i2[...].astype(F32))[0], factor, offset)[1]


def text_kernel(flags, scalars, i3, eu, text, tnorm, tu, gt, grad_out):
    factor, offset = scalars[0], scalars[1]
    passed = to_unit(i3[...].astype(F32))[0].astype(F32)
    third = jnp.where(flags[0] == 1, eu[...].astype(F32), passed).astype(BF16)
    grad = gt[...] + terms(tu[...], third, factor, offset)[1]
    grad_out[...] = project(text[...].astype(F32), tnorm[...], factor * grad)


def near_kernel(flags, scalars, t2, iu, gi, loss_in, gi2, loss_out):
    factor, offset = scalars[0], scalars[1]
    loss, grad = terms(iu[...], to_unit(t2[...].astype(F32))[0], factor, offset)
    gi2[...] = gi[...] + grad
    loss_out[...] = loss_in[...] + loss


def last_kernel(flags, scalars, t3, eu, image, inorm, iu, gi, loss_in, grad_out, loss_out):
    factor, offset = scalars[0], scalars[1]
    passed = to_unit(t3[...].astype(F32))[0].astype(F32)
    third = jnp.where(flags[0] == 1, passed, eu[...].astype(F32)).astype(BF16)
    loss, grad = terms(iu[...], third, factor, offset)
    grad_out[...] = project(image[...].astype(F32), inorm[...], factor * (gi[...] + grad))
    row_loss = (loss_in[...] + loss) * (1.0 / (SPANS * image.shape[0]))
    loss_out[...] = jnp.broadcast_to(row_loss, (row_loss.shape[0], 128)).T[0:1, :]


def call(kernel, outs, pairs, *args, weight=1):
    smem = pl.BlockSpec(memory_space=pltpu.SMEM)
    vmem = pl.BlockSpec(memory_space=pltpu.VMEM)
    rows, depth = 256, 1152
    return pl.pallas_call(
        kernel,
        out_shape=outs,
        in_specs=[smem, smem] + [vmem] * (len(args) - 2),
        out_specs=[vmem] * len(outs),
        compiler_params=pltpu.CompilerParams(vmem_limit_bytes=32 * 2**20),
        cost_estimate=pl.CostEstimate(
            flops=4 * weight * pairs * rows * rows * depth,
            bytes_accessed=8 * rows * depth * 2,
            transcendentals=2 * pairs * rows * rows,
        ),
    )(*args)


def local(image_emb, text_emb, partner, scale, bias):
    rows, depth = image_emb.shape
    even = lax.axis_index("blk") % 2 == 0
    flags = even.astype(jnp.int32).reshape(1)
    scalars = jnp.concatenate([scale, bias])
    half = jax.ShapeDtypeStruct((rows, depth), BF16)
    full = jax.ShapeDtypeStruct((rows, depth), F32)
    col = jax.ShapeDtypeStruct((rows, 1), F32)

    t1 = moved(text_emb, text_far)
    i1 = moved(image_emb, image_far)
    iu, tu, eu, inorm, tnorm, gi, gt, loss = call(
        own_kernel, (half, half, half, col, col, full, full, col), 2,
        flags, scalars, image_emb, text_emb, partner.reshape(rows, 1), partner, weight=10,
    )
    eu = moved(eu, sibling)
    t1, gi = lax.optimization_barrier((t1, gi))
    t2 = moved(t1, text_near)
    i2 = moved(i1, image_near)
    gi, gt, loss = call(
        far_kernel, (full, full, col), 2,
        flags, scalars, t1, i1, iu, tu, gi, gt, loss, weight=10,
    )
    t2, gi = lax.optimization_barrier((t2, gi))
    t3 = moved(t2, text_pass)
    gi, loss = call(
        near_kernel, (full, col), 1, flags, scalars, t2, iu, gi, loss, weight=100
    )
    grad_image, row_loss = call(
        last_kernel, (half, jax.ShapeDtypeStruct((1, rows), F32)), 1,
        flags, scalars, t3, eu, image_emb, inorm, iu, gi, loss, weight=1,
    )
    i2, grad_image = lax.optimization_barrier((i2, grad_image))
    i3 = moved(i2, image_pass)
    (gt,) = call(image_kernel, (full,), 1, flags, scalars, i2, tu, gt, weight=10)
    (grad_text,) = call(
        text_kernel, (half,), 1, flags, scalars, i3, eu, text_emb, tnorm, tu, gt
    )
    return row_loss.reshape(rows), grad_image, grad_text


def solution(mesh):
    rows = P(AXES, None)
    return jax.shard_map(
        local,
        mesh=mesh,
        in_specs=(rows, rows, rows, P(), P()),
        out_specs=(P(AXES), rows, rows),
        check_vma=False,
    )
```

```python
import jax
import jax.numpy as jnp
from jax import lax
from jax.experimental import pallas as pl
from jax.experimental.pallas import tpu as pltpu
from jax.sharding import PartitionSpec as P

SPANS = 4
EPS = 1e-06
AXES = ("blk", "narrow")
F32 = jnp.float32
BF16 = jnp.bfloat16


def moved(block, target):
    rows, cols = lax.axis_size("blk"), lax.axis_size("narrow")
    route = []
    for b in range(rows):
        for n in range(cols):
            to = target(b, n)
            if to is not None:
                route.append((b * cols + n, (to[0] % rows) * cols + to[1] % cols))
    return lax.ppermute(block, AXES, route)


RUN = 8


def text_far(b, n):
    return None if n % RUN == RUN - 1 else (b + 2, n + 1)


def text_near(b, n):
    return None if n % RUN == 0 else (b, n - 1)


def image_far(b, n):
    return None if n % RUN == 0 else (b - 2, n - 1)


def image_near(b, n):
    return None if n % RUN == RUN - 1 else (b, n + 1)


def over_same(b, n):
    return (b + 2, n) if n % RUN == RUN - 1 else (b - 2, n) if n % RUN == 0 else None


def over_next(b, n):
    return (b + 2, n + 1) if n % RUN == RUN - 1 else (b - 2, n - 1) if n % RUN == 0 else None


def over_pass(b, n):
    return text_pass(b, n) if n % RUN == RUN - 1 else image_pass(b, n) if n % RUN == 0 else None


def sibling(b, n):
    return (b ^ 1, n)


def text_pass(b, n):
    return (b - 1, n) if b % 2 else None


def image_pass(b, n):
    return None if b % 2 else (b + 1, n)


def to_unit(values):
    norm = jnp.sqrt(jnp.sum(values * values, axis=-1, keepdims=True) + EPS)
    return (values * (1.0 / norm)).astype(BF16), norm


def terms(fixed, other, factor, offset, positive=None):
    logit = factor * lax.dot_general(
        fixed, other, (((1,), (1,)), ((), ())), preferred_element_type=F32
    ) + offset
    signed = logit if positive is None else jnp.where(positive, -logit, logit)
    small = jnp.exp(-jnp.abs(signed))
    loss = jnp.maximum(signed, 0.0) + jnp.log1p(small)
    share = 1.0 / (1.0 + small)
    weight = jnp.where(signed >= 0.0, share, small * share) * (1.0 / SPANS)
    if positive is not None:
        weight = jnp.where(positive, -weight, weight)
    grad = jnp.dot(weight.astype(BF16), other, preferred_element_type=F32)
    return jnp.sum(loss, axis=-1, keepdims=True), grad


def project(unit_source, norm, grad_unit):
    direction = unit_source * (1.0 / norm)
    along = jnp.sum(direction * grad_unit, axis=-1, keepdims=True)
    return ((grad_unit - direction * along) * (1.0 / norm)).astype(BF16)


def picked(flag, a, b):
    return jnp.where(flag == 1, a[...].astype(F32), b[...].astype(F32))


def own_kernel(
    flags, scalars, image, text, pcol, prow, iu, tu, eu, inorm, tnorm, gi, gt, loss_out
):
    factor, offset = scalars[0], scalars[1]
    even = flags[0] == 1
    i_unit, i_norm = to_unit(image[...].astype(F32))
    t_unit, t_norm = to_unit(text[...].astype(F32))
    shape = (image.shape[0], text.shape[0])
    own = pcol[...] == lax.broadcasted_iota(jnp.int32, shape, 1)
    loss, grad = terms(i_unit, t_unit, factor, offset, own)
    loss_out[...] = loss
    gi[...] = grad
    own = prow[...] == lax.broadcasted_iota(jnp.int32, shape, 0)
    gt[...] = terms(t_unit, i_unit, factor, offset, own)[1]
    iu[...] = i_unit
    tu[...] = t_unit
    inorm[...] = i_norm
    tnorm[...] = t_norm

    @pl.when(even)
    def _():
        eu[...] = t_unit

    @pl.when(jnp.logical_not(even))
    def _():
        eu[...] = i_unit


def far_kernel(flags, scalars, t1, i1, over, iu, tu, gi, gt, loss_in, gi2, gt2, loss_out):
    factor, offset = scalars[0], scalars[1]
    loss, grad = terms(iu[...], to_unit(picked(flags[1], over, t1))[0], factor, offset)
    gi2[...] = gi[...] + grad
    loss_out[...] = loss_in[...] + loss
    gt2[...] = gt[...] + terms(tu[...], to_unit(picked(flags[2], over, i1))[0], factor, offset)[1]


def image_kernel(flags, scalars, i2, over, tu, gt, gt2):
    factor, offset = scalars[0], scalars[1]
    gt2[...] = gt[...] + terms(tu[...], to_unit(picked(flags[1], over, i2))[0], factor, offset)[1]


def text_kernel(flags, scalars, i3, over, eu, text, tnorm, tu, gt, grad_out):
    factor, offset = scalars[0], scalars[1]
    passed = to_unit(picked(flags[1], over, i3))[0].astype(F32)
    third = jnp.where(flags[0] == 1, eu[...].astype(F32), passed).astype(BF16)
    grad = gt[...] + terms(tu[...], third, factor, offset)[1]
    grad_out[...] = project(text[...].astype(F32), tnorm[...], factor * grad)


def near_kernel(flags, scalars, t2, over, iu, gi, loss_in, gi2, loss_out):
    factor, offset = scalars[0], scalars[1]
    loss, grad = terms(iu[...], to_unit(picked(flags[2], over, t2))[0], factor, offset)
    gi2[...] = gi[...] + grad
    loss_out[...] = loss_in[...] + loss


def last_kernel(flags, scalars, t3, over, eu, image, inorm, iu, gi, loss_in, grad_out, loss_out):
    factor, offset = scalars[0], scalars[1]
    passed = to_unit(picked(flags[2], over, t3))[0].astype(F32)
    third = jnp.where(flags[0] == 1, passed, eu[...].astype(F32)).astype(BF16)
    loss, grad = terms(iu[...], third, factor, offset)
    grad_out[...] = project(image[...].astype(F32), inorm[...], factor * (gi[...] + grad))
    row_loss = (loss_in[...] + loss) * (1.0 / (SPANS * image.shape[0]))
    loss_out[...] = jnp.broadcast_to(row_loss, (row_loss.shape[0], 128)).T[0:1, :]


def call(kernel, outs, pairs, *args, weight=1):
    smem = pl.BlockSpec(memory_space=pltpu.SMEM)
    vmem = pl.BlockSpec(memory_space=pltpu.VMEM)
    rows, depth = 256, 1152
    return pl.pallas_call(
        kernel,
        out_shape=outs,
        in_specs=[smem, smem] + [vmem] * (len(args) - 2),
        out_specs=[vmem] * len(outs),
        compiler_params=pltpu.CompilerParams(vmem_limit_bytes=32 * 2**20),
        cost_estimate=pl.CostEstimate(
            flops=4 * weight * pairs * rows * rows * depth,
            bytes_accessed=8 * rows * depth * 2,
            transcendentals=2 * pairs * rows * rows,
        ),
    )(*args)


def local(image_emb, text_emb, partner, scale, bias):
    rows, depth = image_emb.shape
    even = lax.axis_index("blk") % 2 == 0
    place = lax.axis_index("narrow") % RUN
    head, tail = place == 0, place == RUN - 1
    flags = jnp.stack([even, head, tail]).astype(jnp.int32)
    scalars = jnp.concatenate([scale, bias])
    half = jax.ShapeDtypeStruct((rows, depth), BF16)
    full = jax.ShapeDtypeStruct((rows, depth), F32)
    col = jax.ShapeDtypeStruct((rows, 1), F32)

    t1 = moved(text_emb, text_far)
    i1 = moved(image_emb, image_far)
    over = jnp.where(tail, text_emb, image_emb)
    over_d = moved(over, over_same)
    over_c = moved(over, over_next)
    over_p = moved(over_d, over_pass)
    iu, tu, eu, inorm, tnorm, gi, gt, loss = call(
        own_kernel, (half, half, half, col, col, full, full, col), 2,
        flags, scalars, image_emb, text_emb, partner.reshape(rows, 1), partner, weight=10,
    )
    eu = moved(eu, sibling)
    t1, gi = lax.optimization_barrier((t1, gi))
    t2 = moved(t1, text_near)
    i2 = moved(i1, image_near)
    gi, gt, loss = call(
        far_kernel, (full, full, col), 2,
        flags, scalars, t1, i1, over_c, iu, tu, gi, gt, loss, weight=10,
    )
    t2, gi = lax.optimization_barrier((t2, gi))
    t3 = moved(t2, text_pass)
    gi, loss = call(
        near_kernel, (full, col), 1, flags, scalars, t2, over_d, iu, gi, loss, weight=100
    )
    grad_image, row_loss = call(
        last_kernel, (half, jax.ShapeDtypeStruct((1, rows), F32)), 1,
        flags, scalars, t3, over_p, eu, image_emb, inorm, iu, gi, loss, weight=1,
    )
    i2, grad_image = lax.optimization_barrier((i2, grad_image))
    i3 = moved(i2, image_pass)
    (gt,) = call(image_kernel, (full,), 1, flags, scalars, i2, over_d, tu, gt, weight=10)
    (grad_text,) = call(
        text_kernel, (half,), 1, flags, scalars, i3, over_p, eu, text_emb, tnorm, tu, gt
    )
    return row_loss.reshape(rows), grad_image, grad_text


def solution(mesh):
    rows = P(AXES, None)
    return jax.shard_map(
        local,
        mesh=mesh,
        in_specs=(rows, rows, rows, P(), P()),
        out_specs=(P(AXES), rows, rows),
        check_vma=False,
    )
```

```python
import jax
import jax.numpy as jnp
from jax import lax
from jax.experimental import pallas as pl
from jax.experimental.pallas import tpu as pltpu
from jax.sharding import PartitionSpec as P

SPANS = 4
EPS = 1e-06
AXES = ("blk", "narrow")
F32 = jnp.float32
BF16 = jnp.bfloat16


def moved(block, target):
    rows, cols = lax.axis_size("blk"), lax.axis_size("narrow")
    route = []
    for b in range(rows):
        for n in range(cols):
            to = target(b, n)
            if to is not None:
                route.append((b * cols + n, (to[0] % rows) * cols + to[1] % cols))
    return lax.ppermute(block, AXES, route)


def text_far(b, n):
    return (b + 2, n + 1)


def text_near(b, n):
    return (b, n - 1)


def image_far(b, n):
    return (b - 2, n - 1)


def image_near(b, n):
    return (b, n + 1)


def sibling(b, n):
    return (b ^ 1, n)


def text_pass(b, n):
    return (b - 1, n) if b % 2 else None


def image_pass(b, n):
    return None if b % 2 else (b + 1, n)


def to_unit(values):
    norm = jnp.sqrt(jnp.sum(values * values, axis=-1, keepdims=True) + EPS)
    return (values * (1.0 / norm)).astype(BF16), norm


def terms(fixed, other, factor, offset, positive=None):
    logit = factor * lax.dot_general(
        fixed, other, (((1,), (1,)), ((), ())), preferred_element_type=F32
    ) + offset
    signed = logit if positive is None else jnp.where(positive, -logit, logit)
    small = jnp.exp(-jnp.abs(signed))
    loss = jnp.maximum(signed, 0.0) + jnp.log1p(small)
    share = 1.0 / (1.0 + small)
    weight = jnp.where(signed >= 0.0, share, small * share) * (1.0 / SPANS)
    if positive is not None:
        weight = jnp.where(positive, -weight, weight)
    grad = jnp.dot(weight.astype(BF16), other, preferred_element_type=F32)
    return jnp.sum(loss, axis=-1, keepdims=True), grad


def project(source, norm, grad_unit):
    scale = 1.0 / norm
    along = jnp.sum(source * grad_unit, axis=-1, keepdims=True) * scale * scale
    return ((grad_unit - source * along) * scale).astype(BF16)


def own_kernel(
    flags, scalars, image, text, pcol, prow, iu, tu, eu, inorm, tnorm, gi, gt, loss_out
):
    factor, offset = scalars[0], scalars[1]
    even = flags[0] == 1
    i_unit, i_norm = to_unit(image[...].astype(F32))
    t_unit, t_norm = to_unit(text[...].astype(F32))
    shape = (image.shape[0], text.shape[0])
    own = pcol[...] == lax.broadcasted_iota(jnp.int32, shape, 1)
    loss, grad = terms(i_unit, t_unit, factor, offset, own)
    loss_out[...] = loss
    gi[...] = grad
    own = prow[...] == lax.broadcasted_iota(jnp.int32, shape, 0)
    gt[...] = terms(t_unit, i_unit, factor, offset, own)[1]
    iu[...] = i_unit
    tu[...] = t_unit
    inorm[...] = i_norm
    tnorm[...] = t_norm

    @pl.when(even)
    def _():
        eu[...] = t_unit

    @pl.when(jnp.logical_not(even))
    def _():
        eu[...] = i_unit


def far_kernel(flags, scalars, t1, i1, iu, tu, gi, gt, loss_in, gi2, gt2, loss_out):
    factor, offset = scalars[0], scalars[1]
    loss, grad = terms(iu[...], to_unit(t1[...].astype(F32))[0], factor, offset)
    gi2[...] = gi[...] + grad
    loss_out[...] = loss_in[...] + loss
    gt2[...] = gt[...] + terms(tu[...], to_unit(i1[...].astype(F32))[0], factor, offset)[1]


def image_kernel(flags, scalars, i2, tu, gt, gt2):
    factor, offset = scalars[0], scalars[1]
    gt2[...] = gt[...] + terms(tu[...], to_unit(i2[...].astype(F32))[0], factor, offset)[1]


def text_kernel(flags, scalars, i3, eu, text, tnorm, tu, gt, grad_out):
    factor, offset = scalars[0], scalars[1]
    third = jnp.where(flags[0] == 1, eu[...], to_unit(i3[...].astype(F32))[0])
    grad = gt[...] + terms(tu[...], third, factor, offset)[1]
    grad_out[...] = project(text[...].astype(F32), tnorm[...], factor * grad)


def near_kernel(flags, scalars, t2, iu, gi, loss_in, gi2, loss_out):
    factor, offset = scalars[0], scalars[1]
    loss, grad = terms(iu[...], to_unit(t2[...].astype(F32))[0], factor, offset)
    gi2[...] = gi[...] + grad
    loss_out[...] = loss_in[...] + loss


def last_kernel(flags, scalars, t3, eu, image, inorm, iu, gi, loss_in, grad_out, loss_out):
    factor, offset = scalars[0], scalars[1]
    third = jnp.where(flags[0] == 1, to_unit(t3[...].astype(F32))[0], eu[...])
    loss, grad = terms(iu[...], third, factor, offset)
    grad_out[...] = project(image[...].astype(F32), inorm[...], factor * (gi[...] + grad))
    row_loss = (loss_in[...] + loss) * (1.0 / (SPANS * image.shape[0]))
    loss_out[...] = jnp.broadcast_to(row_loss, (row_loss.shape[0], 128)).T[0:1, :]


def call(kernel, outs, pairs, *args, weight=1):
    smem = pl.BlockSpec(memory_space=pltpu.SMEM)
    vmem = pl.BlockSpec(memory_space=pltpu.VMEM)
    rows, depth = 256, 1152
    return pl.pallas_call(
        kernel,
        out_shape=outs,
        in_specs=[smem, smem] + [vmem] * (len(args) - 2),
        out_specs=[vmem] * len(outs),
        compiler_params=pltpu.CompilerParams(vmem_limit_bytes=32 * 2**20),
        cost_estimate=pl.CostEstimate(
            flops=4 * weight * pairs * rows * rows * depth,
            bytes_accessed=8 * rows * depth * 2,
            transcendentals=2 * pairs * rows * rows,
        ),
    )(*args)


def local(image_emb, text_emb, partner, scale, bias):
    rows, depth = image_emb.shape
    even = lax.axis_index("blk") % 2 == 0
    flags = even.astype(jnp.int32).reshape(1)
    scalars = jnp.concatenate([scale, bias])
    half = jax.ShapeDtypeStruct((rows, depth), BF16)
    full = jax.ShapeDtypeStruct((rows, depth), F32)
    col = jax.ShapeDtypeStruct((rows, 1), F32)

    t1 = moved(text_emb, text_far)
    i1 = moved(image_emb, image_far)
    iu, tu, eu, inorm, tnorm, gi, gt, loss = call(
        own_kernel, (half, half, half, col, col, full, full, col), 2,
        flags, scalars, image_emb, text_emb, partner.reshape(rows, 1), partner, weight=10,
    )
    eu = moved(eu, sibling)
    t1, gi = lax.optimization_barrier((t1, gi))
    t2 = moved(t1, text_near)
    i2 = moved(i1, image_near)
    gi, gt, loss = call(
        far_kernel, (full, full, col), 2,
        flags, scalars, t1, i1, iu, tu, gi, gt, loss, weight=10,
    )
    t2, gi = lax.optimization_barrier((t2, gi))
    t3 = moved(t2, text_pass)
    gi, loss = call(
        near_kernel, (full, col), 1, flags, scalars, t2, iu, gi, loss, weight=100
    )
    grad_image, row_loss = call(
        last_kernel, (half, jax.ShapeDtypeStruct((1, rows), F32)), 1,
        flags, scalars, t3, eu, image_emb, inorm, iu, gi, loss, weight=1,
    )
    i2, grad_image = lax.optimization_barrier((i2, grad_image))
    i3 = moved(i2, image_pass)
    (gt,) = call(image_kernel, (full,), 1, flags, scalars, i2, tu, gt, weight=10)
    (grad_text,) = call(
        text_kernel, (half,), 1, flags, scalars, i3, eu, text_emb, tnorm, tu, gt
    )
    return row_loss.reshape(rows), grad_image, grad_text


def solution(mesh):
    rows = P(AXES, None)
    return jax.shard_map(
        local,
        mesh=mesh,
        in_specs=(rows, rows, rows, P(), P()),
        out_specs=(P(AXES), rows, rows),
        check_vma=False,
    )
```
